32 devices in a mesh: row: 16 (over z, x, core), blk: 2 (over y).
Axes of the slice: x: 2, y: 2, z: 4, core: 2. Of those that a mesh axis runs over, the one named last changes fastest.
Arguments:
- factor_panel: bfloat16 [32768, 2, 2048], P('row', None, 'blk'), may hold values from -0.09375 to 0.09375
- right_side: float32 [256, 32768], P('blk', 'row'), may hold values from -6 to 6
- block_inverse: float32 [2, 2048, 2048], P(None, 'row', 'blk'), may hold values from -2 to 2, as said below
Outputs:
- solved: float32 [2, 256, 2048], P(None, 'blk', 'row')
- reduced_side: float32 [256, 32768], P('blk', 'row')
The draws below stay inside these ranges and needn't reach their ends.
Inputs may be any that keep to these rules, and one draw needn't show every extreme that they name: block_inverse[k] is lower triangular with diagonal entries between 1 and 2.
All inputs are finite; a program needn't handle non-finite values.
Results may differ from the reference program's by a relative error of at most 0.015.
Values may be sent and summed in bfloat16 or wider, within the bound.
A program may use at most 64 MiB of HBM per device.

```python
import jax
import jax.numpy as jnp
from jax import lax

NB = 2048
STEPS = 2
DATES = 256
ORDER = 32768
N_BLK = 2


def draw_block_inverse(key, part):
    key_off = jax.random.fold_in(key, 11)
    key_diag = jax.random.fold_in(key, 12)
    scale = 0.5 / NB ** 0.5
    lower = jnp.clip(jax.random.normal(key_off, (STEPS, NB, NB), jnp.float32), -4.0, 4.0) * scale
    diag = jax.random.uniform(key_diag, (STEPS, NB, NB), jnp.float32, 1.0, 2.0)
    rows = jnp.arange(NB)[:, None]
    cols = jnp.arange(NB)[None, :]
    return jnp.where(rows > cols, lower, jnp.where(rows == cols, diag, jnp.float32(0.0)))


def shard_levels(key, shape, cuts, least, largest):
    def one(position, shards_of):
        draws = jax.random.uniform(jax.random.fold_in(jax.random.fold_in(key, 6), position), (shards_of,), jnp.float32, least / len(cuts), largest / len(cuts))
        return jnp.repeat(jnp.exp(draws), shape[position] // shards_of).reshape((-1,) + (1,) * (len(shape) - position - 1))

    level = one(*cuts[0])
    for cut in cuts[1:]:
        level = level * one(*cut)
    return level


def noise(rng, extent, deviation, bound, cuts=(), kind=jnp.bfloat16):
    array = jax.random.normal(rng, extent, jnp.float32) * deviation
    if len(cuts) > 0:
        array = shard_levels(rng, extent, cuts, -0.22, 0.18) * array
    return jnp.clip(array, min=-bound, max=bound).astype(kind)


def setup_inputs(seed: int = 0) -> dict:
    seeds = jax.random.split(jax.random.key(seed), 4)
    factor_panel = noise(seeds[0], (ORDER, STEPS, NB), (2 * NB) ** -0.5, 0.09375, ((0, 16), (2, 2)))
    right_side = noise(seeds[1], (DATES, ORDER), 1.0, 6.0, ((0, 2), (1, 16)), jnp.float32)
    block_inverse = draw_block_inverse(jax.random.fold_in(seeds[3], 71), 0)
    return dict(factor_panel=factor_panel, right_side=right_side, block_inverse=block_inverse)


def reference(factor_panel, right_side, block_inverse):
    reduced_side = right_side
    column_index = jnp.arange(ORDER, dtype=jnp.int32)
    width = NB // N_BLK
    outputs = []
    for section in range(STEPS):
        pivot_rows = lax.dynamic_slice_in_dim(reduced_side, section * NB, NB, 1)
        solved_now = jnp.dot(pivot_rows, block_inverse[section].T, precision=lax.Precision.HIGHEST)
        outputs.append(solved_now)
        solved_half = solved_now.astype(jnp.bfloat16).astype(jnp.float32)
        panel_now = factor_panel[:, section, :].astype(jnp.float32)
        update = jnp.zeros((DATES, ORDER), jnp.float32)
        for group in range(N_BLK):
            left = solved_half[:, group * width:(group + 1) * width]
            right = panel_now[:, group * width:(group + 1) * width]
            term = jnp.dot(left, right.T, precision=lax.Precision.HIGHEST)
            term = lax.optimization_barrier(term.astype(jnp.bfloat16))
            update = update + term.astype(jnp.float32)
        below = (column_index >= (section + 1) * NB)[None, :]
        reduced_side = reduced_side - jnp.where(below, update, jnp.float32(0.0))
    return jnp.stack(outputs), reduced_side
```

```python
import functools

import jax
import jax.numpy as jnp
from jax import lax
from jax.experimental import pallas as pl
from jax.experimental.pallas import tpu as pltpu
from jax.sharding import PartitionSpec as P

MESH = pl.DeviceIdType.MESH
BF16 = jnp.bfloat16
F32 = jnp.float32


def dot_t(a, b):
    return lax.dot_general(a, b, (((1,), (1,)), ((), ())), preferred_element_type=F32)


def kernel(
    n_row, n_blk, cw, cu, cs,
    panel_hbm, right_ref, inverse_ref,
    solved_ref, reduced_ref,
    panel_raw, panel, own_inverse, inverse, side, own_solved, blocks, solved_full, total,
    update_out, update_in,
    panel_sem, inv_send, inv_recv, side_send, side_recv,
    hop_send, hop_recv, line_send, cross_send, core_send, block_recv, upd_send, upd_recv,
):
    row, blk = lax.axis_index("row"), lax.axis_index("blk")
    dates, pixels = right_ref.shape
    steps, width, group = inverse_ref.shape
    chunks = side.shape[1]
    per = n_row // n_blk
    line = n_row // 4
    zz, xx, core = row // 4, lax.rem(row // 2, 2), lax.rem(row, 2)
    chip = row // 2
    cross_row = row + 2 - 4 * xx
    core_row = row + 1 - 2 * core
    my_group = row // per
    my_slot = lax.rem(row, per)
    my_dates = pl.ds(pl.multiple_of(blk * dates, dates), dates)
    n_upd = pixels // cu

    def at_blk(j):
        return lax.rem(blk + j, n_blk)

    def copy_to(src, dst, send, recv, to_row, to_blk):
        return pltpu.make_async_remote_copy(
            src_ref=src, dst_ref=dst, send_sem=send, recv_sem=recv,
            device_id=(to_row, to_blk), device_id_type=MESH,
        )

    load = pltpu.make_async_copy(panel_hbm, panel_raw, panel_sem)
    load.start()

    barrier = pltpu.get_barrier_semaphore()

    def greet(to_row, to_blk):
        pl.semaphore_signal(barrier, inc=1, device_id=(to_row, to_blk), device_id_type=MESH)

    greet(core_row, blk)
    greet(cross_row, blk)
    for d in range(1, line):
        greet(lax.rem(row + 4 * d, n_row), blk)
    for j in range(1, n_blk):
        greet(row, at_blk(j))

    for s in range(steps):
        own_inverse[s] = inverse_ref[s].astype(BF16)

    @pl.when(row == 0)
    def _():
        for i in range(chunks):
            side[0, i] = right_ref[:, i * cw:(i + 1) * cw].astype(BF16)

    pl.semaphore_wait(barrier, 1 + 1 + (line - 1) + (n_blk - 1))

    def inverse_copy(s, j):
        return copy_to(
            own_inverse.at[s], inverse.at[s, blk], inv_send.at[s, j], inv_recv.at[s, blk], row, at_blk(j)
        )

    def inverse_wait(s, j):
        return copy_to(
            own_inverse.at[s], inverse.at[s, at_blk(j)], inv_send.at[s, j], inv_recv.at[s, at_blk(j)],
            row, at_blk(j),
        )

    def side_sends(s, i):
        half = lax.rem(i, 2)
        lane = core == s
        own = xx == half
        ref, recv = side.at[s, i], side_recv.at[s, i]
        down = copy_to(ref, ref, side_send.at[s, i, 0], recv, lax.rem(row + 4, n_row), blk)
        across = copy_to(ref, ref, side_send.at[s, i, 1], recv, cross_row, blk)
        over = copy_to(ref, ref, side_send.at[s, i, 2], recv, core_row, blk)
        return (
            (lane & own & (zz < line - 1), down),
            (lane & ((own & (chip != 1)) | (chip == 0)), across),
            (lane, over),
        )

    def side_start(s, i):
        for need, copy in side_sends(s, i):
            @pl.when(need)
            def _():
                copy.start()

    def side_finish(s):
        def body(i, carry):
            for need, copy in side_sends(s, i):
                @pl.when(need)
                def _():
                    copy.wait_send()
            return carry
        lax.fori_loop(0, chunks, body, 0)

    def side_wait(s, i):
        copy_to(side.at[s, i], side.at[s, i], side_send.at[s, i, 0], side_recv.at[s, i], core_row, blk).wait_recv()

    def split(s, i):
        rows = pl.ds(pl.multiple_of(i * cs, cs), cs)
        pair = panel_raw[rows].reshape(2 * cs, group)
        r = lax.broadcasted_iota(jnp.int32, (cs, 2 * cs), 0)
        c = lax.broadcasted_iota(jnp.int32, (cs, 2 * cs), 1)
        pick = jnp.where(c == 2 * r + s, 1.0, 0.0).astype(BF16)
        panel[s, rows, :] = jnp.dot(pick, pair, preferred_element_type=F32).astype(BF16)

    n_split = pixels // cs // chunks

    def side_stage(s):
        def body(i, carry):
            @pl.when(row != s)
            def _():
                side_wait(s, i)
                side_start(s, i)

            @pl.when(row > s)
            def _():
                @pl.when(i == 0)
                def _():
                    if s == 0:
                        load.wait()
                for m in range(n_split):
                    split(s, i * n_split + m)
            return carry
        lax.fori_loop(0, chunks, body, 0)

    def hop(s):
        return copy_to(
            own_solved.at[s], blocks.at[s, my_slot, my_dates], hop_send.at[s], hop_recv.at[s, blk], row, my_group
        )

    def hop_in(s, j):
        src = at_blk(j)
        where = pl.ds(pl.multiple_of(src * dates, dates), dates)
        return copy_to(
            own_solved.at[s], blocks.at[s, my_slot, where], hop_send.at[s], hop_recv.at[s, src], row, src
        )

    def block_copy(s, slot, send, to_row):
        ref = blocks.at[s, slot]
        return copy_to(ref, ref, send, block_recv.at[s, slot], to_row, blk)

    def line_copy(s, d):
        return block_copy(s, my_slot, line_send.at[s, d], lax.rem(row + 4 * d, n_row))

    def cross_copy(s, slot):
        return block_copy(s, slot, cross_send.at[s, slot], cross_row)

    def core_copy(s, slot):
        return block_copy(s, slot, core_send.at[s, slot], core_row)

    def solve_stage(s):
        for j in range(1, n_blk):
            inverse_wait(s, j).wait_recv()
        inverse[s, blk] = own_inverse[s]
        value = jnp.zeros((dates, width), F32)
        for i in range(chunks):
            at, off = (i * cw) // group, (i * cw) % group
            value = value + dot_t(side[s, i], inverse[s, at, :, off:off + cw])
        solved_ref[s] = value
        half = value.astype(BF16)

        @pl.when(blk != my_group)
        def _():
            own_solved[s] = half
            hop(s).start()

        @pl.when(blk == my_group)
        def _():
            blocks[s, my_slot, my_dates] = half

        if s + 1 < steps:
            for j in range(1, n_blk):
                inverse_copy(s + 1, j).start()

        @pl.when(blk == my_group)
        def _():
            for j in range(1, n_blk):
                hop_in(s, j).wait_recv()
            for d in range(1, line):
                line_copy(s, d).start()
            cross_copy(s, my_slot).start()
            core_copy(s, my_slot).start()

        for turn in range(4):
            x_of = xx if turn % 2 == 0 else 1 - xx
            c_of = core if turn < 2 else 1 - core
            for a in range(per // 4):
                slot = 4 * a + 2 * x_of + c_of
                mine = (blk == my_group) & (slot == my_slot)

                @pl.when(jnp.logical_not(mine))
                def _():
                    block_copy(s, slot, core_send.at[s, slot], core_row).wait_recv()
                    if turn == 0:
                        cross_copy(s, slot).start()
                    if turn < 2:
                        core_copy(s, slot).start()
        solved_full[...] = jnp.concatenate([blocks[s, t] for t in range(per)], axis=1)

    def solve_finish(s):
        @pl.when(blk != my_group)
        def _():
            hop(s).wait_send()

        @pl.when(blk == my_group)
        def _():
            for d in range(1, line):
                line_copy(s, d).wait_send()
        for turn in range(2):
            x_of = xx if turn % 2 == 0 else 1 - xx
            for a in range(per // 4):
                slot = 4 * a + 2 * x_of + core
                if turn == 0:
                    cross_copy(s, slot).wait_send()
                core_copy(s, slot).wait_send()

    def update_copy(i, j):
        return copy_to(
            update_out.at[j, i], update_in.at[blk, i], upd_send.at[j, i], upd_recv.at[blk, i], row, at_blk(j)
        )

    def update_wait(i, j):
        src = at_blk(j)
        return copy_to(
            update_out.at[j, i], update_in.at[src, i], upd_send.at[j, i], upd_recv.at[src, i], row, src
        )

    def pixel_part(i):
        return pl.ds(pl.multiple_of(i * cu, cu), cu)

    def update_out_stage(s, add):
        def body(i, carry):
            cols = pixel_part(i)
            term = dot_t(solved_full[...], panel[s, cols, :])
            if add:
                term = term + total[:, cols]
            total[:, cols] = term
            for j in range(1, n_blk):
                theirs = pl.ds(pl.multiple_of(at_blk(j) * dates, dates), dates)
                update_out[j, i] = total[theirs, cols].astype(BF16)
                update_copy(i, j).start()
            return carry
        lax.fori_loop(0, n_upd, body, 0)

    def reduced_part(i):
        cols = pixel_part(i)
        value = right_ref[:, cols] - total[my_dates, cols]
        for j in range(1, n_blk):
            update_wait(i, j).wait_recv()
            value = value - update_in[at_blk(j), i].astype(F32)
        reduced_ref[:, cols] = value
        return value

    @pl.when(row == 0)
    def _():
        lax.fori_loop(0, chunks, lambda i, c: (side_start(0, i), c)[1], 0)

    for j in range(1, n_blk):
        inverse_copy(0, j).start()

    side_stage(0)
    solve_stage(0)

    @pl.when(row == 0)
    def _():
        load.wait()
        reduced_ref[...] = right_ref[...]

    @pl.when(row == 1)
    def _():
        update_out_stage(0, False)

        def body(i, carry):
            side[1, i] = reduced_part(i).astype(BF16)
            side_start(1, i)
            return carry
        lax.fori_loop(0, n_upd, body, 0)

    @pl.when(row > 1)
    def _():
        def body(i, carry):
            cols = pixel_part(i)
            total[:, cols] = dot_t(solved_full[...], panel[0, cols, :])
            return carry
        lax.fori_loop(0, n_upd, body, 0)

    side_stage(1)
    solve_stage(1)

    @pl.when(row > 1)
    def _():
        update_out_stage(1, True)

        def body(i, carry):
            reduced_part(i)
            return carry
        lax.fori_loop(0, n_upd, body, 0)

    for s in range(steps):
        for j in range(1, n_blk):
            inverse_copy(s, j).wait_send()
        side_finish(s)
        solve_finish(s)

    @pl.when(row > 0)
    def _():
        def body(i, carry):
            for j in range(1, n_blk):
                update_copy(i, j).wait_send()
            return carry
        lax.fori_loop(0, n_upd, body, 0)


def solution(mesh):
    n_row, n_blk = mesh.shape["row"], mesh.shape["blk"]

    def local(factor_panel, right_side, block_inverse):
        pixels, steps, group = factor_panel.shape
        dates = right_side.shape[0]
        width = block_inverse.shape[1]
        order = group * n_blk
        cw = min(256, group)
        chunks = order // cw
        cu, cs = cw, 128
        n_upd = pixels // cu
        per, line = n_row // n_blk, n_row // 4
        dma = pltpu.SemaphoreType.DMA
        return pl.pallas_call(
            functools.partial(kernel, n_row, n_blk, cw, cu, cs),
            out_shape=(
                jax.ShapeDtypeStruct((steps, dates, width), F32),
                jax.ShapeDtypeStruct((dates, pixels), F32),
            ),
            in_specs=[
                pl.BlockSpec(memory_space=pl.ANY),
                pl.BlockSpec(memory_space=pltpu.VMEM),
                pl.BlockSpec(memory_space=pltpu.VMEM),
            ],
            out_specs=(
                pl.BlockSpec(memory_space=pltpu.VMEM),
                pl.BlockSpec(memory_space=pltpu.VMEM),
            ),
            scratch_shapes=[
                pltpu.VMEM((pixels, steps, group), BF16),
                pltpu.VMEM((steps, pixels, group), BF16),
                pltpu.VMEM((steps, width, group), BF16),
                pltpu.VMEM((steps, n_blk, width, group), BF16),
                pltpu.VMEM((steps, chunks, dates, cw), BF16),
                pltpu.VMEM((steps, dates, width), BF16),
                pltpu.VMEM((steps, per, n_blk * dates, width), BF16),
                pltpu.VMEM((n_blk * dates, group), BF16),
                pltpu.VMEM((n_blk * dates, pixels), F32),
                pltpu.VMEM((n_blk, n_upd, dates, cu), BF16),
                pltpu.VMEM((n_blk, n_upd, dates, cu), BF16),
                dma,
                dma((steps, n_blk)),
                dma((steps, n_blk)),
                dma((steps, chunks, 3)),
                dma((steps, chunks)),
                dma((steps,)),
                dma((steps, n_blk)),
                dma((steps, line)),
                dma((steps, per)),
                dma((steps, per)),
                dma((steps, per)),
                dma((n_blk, n_upd)),
                dma((n_blk, n_upd)),
            ],
            compiler_params=pltpu.CompilerParams(
                collective_id=0, has_side_effects=True, vmem_limit_bytes=48 << 20
            ),
        )(factor_panel, right_side, block_inverse)

    return jax.shard_map(
        local,
        mesh=mesh,
        in_specs=(P("row", None, "blk"), P("blk", "row"), P(None, "row", "blk")),
        out_specs=(P(None, "blk", "row"), P("blk", "row")),
        check_vma=False,
    )
```

```python
import functools

import jax
import jax.numpy as jnp
from jax import lax
from jax.experimental import pallas as pl
from jax.experimental.pallas import tpu as pltpu
from jax.sharding import PartitionSpec as P

MESH = pl.DeviceIdType.MESH
BF16 = jnp.bfloat16
F32 = jnp.float32


def dot_t(a, b):
    return lax.dot_general(a, b, (((1,), (1,)), ((), ())), preferred_element_type=F32)


def kernel(
    n_row, n_blk, cw, cu, cs,
    panel_hbm, right_ref, inverse_ref,
    solved_ref, reduced_ref,
    panel_raw, panel, own_inverse, inverse, side, own_solved, blocks, solved_full, total,
    update_out, update_in,
    panel_sem, inv_send, inv_recv, side_send, side_recv,
    hop_send, hop_recv, line_send, cross_send, core_send, block_recv, upd_send, upd_recv,
):
    row, blk = lax.axis_index("row"), lax.axis_index("blk")
    dates, pixels = right_ref.shape
    steps, width, group = inverse_ref.shape
    chunks = side.shape[1]
    per = n_row // n_blk
    line = n_row // 4
    zz, xx, core = row // 4, lax.rem(row // 2, 2), lax.rem(row, 2)
    chip = row // 2
    cross_row = row + 2 - 4 * xx
    core_row = row + 1 - 2 * core
    my_group = row // per
    my_slot = lax.rem(row, per)
    my_dates = pl.ds(pl.multiple_of(blk * dates, dates), dates)
    n_upd = pixels // cu

    def at_blk(j):
        return lax.rem(blk + j, n_blk)

    def copy_to(src, dst, send, recv, to_row, to_blk):
        return pltpu.make_async_remote_copy(
            src_ref=src, dst_ref=dst, send_sem=send, recv_sem=recv,
            device_id=(to_row, to_blk), device_id_type=MESH,
        )

    load = pltpu.make_async_copy(panel_hbm, panel_raw, panel_sem)
    load.start()

    barrier = pltpu.get_barrier_semaphore()

    def greet(to_row, to_blk):
        pl.semaphore_signal(barrier, inc=1, device_id=(to_row, to_blk), device_id_type=MESH)

    greet(core_row, blk)
    greet(cross_row, blk)
    for d in range(1, line):
        greet(lax.rem(row + 4 * d, n_row), blk)
    for j in range(1, n_blk):
        greet(row, at_blk(j))

    for s in range(steps):
        own_inverse[s] = inverse_ref[s].astype(BF16)

    @pl.when(row == 0)
    def _():
        for i in range(chunks):
            side[0, i] = right_ref[:, i * cw:(i + 1) * cw].astype(BF16)

    pl.semaphore_wait(barrier, 1 + 1 + (line - 1) + (n_blk - 1))

    def holds(j):
        return j * group < 2 * width * (chip + 1)

    def inverse_start(s):
        for j in range(1, n_blk):
            @pl.when(holds(blk))
            def _():
                inverse_copy(s, j).start()

    def inverse_finish(s):
        for j in range(1, n_blk):
            @pl.when(holds(blk))
            def _():
                inverse_copy(s, j).wait_send()

    def inverse_arrive(s):
        for j in range(1, n_blk):
            @pl.when(holds(at_blk(j)))
            def _():
                inverse_wait(s, j).wait_recv()

    def inverse_copy(s, j):
        return copy_to(
            own_inverse.at[s], inverse.at[s, blk], inv_send.at[s, j], inv_recv.at[s, blk], row, at_blk(j)
        )

    def inverse_wait(s, j):
        return copy_to(
            own_inverse.at[s], inverse.at[s, at_blk(j)], inv_send.at[s, j], inv_recv.at[s, at_blk(j)],
            row, at_blk(j),
        )

    def needs(chip_of, i):
        return i * cw < 2 * width * (chip_of + 1)

    def side_sends(s, i):
        half = lax.rem(i, 2)
        lane = core == s
        own = xx == half
        ref, recv = side.at[s, i], side_recv.at[s, i]
        down = copy_to(ref, ref, side_send.at[s, i, 0], recv, lax.rem(row + 4, n_row), blk)
        across = copy_to(ref, ref, side_send.at[s, i, 1], recv, cross_row, blk)
        over = copy_to(ref, ref, side_send.at[s, i, 2], recv, core_row, blk)
        there = own & (chip != 1) & needs(chip + 1 - 2 * xx, i)
        return (
            (lane & own & (zz < line - 1), down),
            (lane & (there | ((chip == 0) & jnp.logical_not(own))), across),
            (lane & needs(chip, i), over),
        )

    def side_start(s, i):
        for need, copy in side_sends(s, i):
            @pl.when(need)
            def _():
                copy.start()

    def side_finish(s):
        def body(i, carry):
            for need, copy in side_sends(s, i):
                @pl.when(need)
                def _():
                    copy.wait_send()
            return carry
        lax.fori_loop(0, chunks, body, 0)

    def side_wait(s, i):
        copy_to(side.at[s, i], side.at[s, i], side_send.at[s, i, 0], side_recv.at[s, i], core_row, blk).wait_recv()

    def split(s, i):
        rows = pl.ds(pl.multiple_of(i * cs, cs), cs)
        pair = panel_raw[rows].reshape(2 * cs, group)
        r = lax.broadcasted_iota(jnp.int32, (cs, 2 * cs), 0)
        c = lax.broadcasted_iota(jnp.int32, (cs, 2 * cs), 1)
        pick = jnp.where(c == 2 * r + s, 1.0, 0.0).astype(BF16)
        panel[s, rows, :] = jnp.dot(pick, pair, preferred_element_type=F32).astype(BF16)

    n_split = pixels // cs // chunks

    def side_stage(s):
        def turn(own):
            def body(m, carry):
                i = 2 * m + (xx if own else 1 - xx)
                lane = core == s
                due = needs(chip, i) | (lane if own else False)

                @pl.when((row != s) & due)
                def _():
                    side_wait(s, i)
                    side_start(s, i)

                @pl.when(row > s)
                def _():
                    if s == 0 and own:
                        @pl.when(m == 0)
                        def _():
                            load.wait()
                    base = (m if own else m + chunks // 2) * n_split
                    for k in range(n_split):
                        split(s, base + k)
                return carry
            lax.fori_loop(0, chunks // 2, body, 0)
        turn(True)
        turn(False)

    def hop(s):
        return copy_to(
            own_solved.at[s], blocks.at[s, my_slot, my_dates], hop_send.at[s], hop_recv.at[s, blk], row, my_group
        )

    def hop_in(s, j):
        src = at_blk(j)
        where = pl.ds(pl.multiple_of(src * dates, dates), dates)
        return copy_to(
            own_solved.at[s], blocks.at[s, my_slot, where], hop_send.at[s], hop_recv.at[s, src], row, src
        )

    def block_copy(s, slot, send, to_row):
        ref = blocks.at[s, slot]
        return copy_to(ref, ref, send, block_recv.at[s, slot], to_row, blk)

    def line_copy(s, d):
        return block_copy(s, my_slot, line_send.at[s, d], lax.rem(row + 4 * d, n_row))

    def cross_copy(s, slot):
        return block_copy(s, slot, cross_send.at[s, slot], cross_row)

    def core_copy(s, slot):
        return block_copy(s, slot, core_send.at[s, slot], core_row)

    def solve_stage(s):
        inverse_arrive(s)
        inverse[s, blk] = own_inverse[s]
        solved_ref[s] = jnp.zeros((dates, width), F32)
        for i in range(chunks):
            at, off = (i * cw) // group, (i * cw) % group

            @pl.when(needs(chip, i))
            def _():
                solved_ref[s] = solved_ref[s] + dot_t(side[s, i], inverse[s, at, :, off:off + cw])
        half = solved_ref[s].astype(BF16)

        @pl.when(blk != my_group)
        def _():
            own_solved[s] = half
            hop(s).start()

        @pl.when(blk == my_group)
        def _():
            blocks[s, my_slot, my_dates] = half

        if s + 1 < steps:
            inverse_start(s + 1)

        @pl.when(blk == my_group)
        def _():
            for j in range(1, n_blk):
                hop_in(s, j).wait_recv()
            for d in range(1, line):
                line_copy(s, d).start()
            cross_copy(s, my_slot).start()
            core_copy(s, my_slot).start()

        for turn in range(4):
            x_of = xx if turn % 2 == 0 else 1 - xx
            c_of = core if turn < 2 else 1 - core
            for a in range(per // 4):
                slot = 4 * a + 2 * x_of + c_of
                mine = (blk == my_group) & (slot == my_slot)

                @pl.when(jnp.logical_not(mine))
                def _():
                    block_copy(s, slot, core_send.at[s, slot], core_row).wait_recv()
                    if turn == 0:
                        cross_copy(s, slot).start()
                    if turn < 2:
                        core_copy(s, slot).start()
        solved_full[...] = jnp.concatenate([blocks[s, t] for t in range(per)], axis=1)

    def solve_finish(s):
        @pl.when(blk != my_group)
        def _():
            hop(s).wait_send()

        @pl.when(blk == my_group)
        def _():
            for d in range(1, line):
                line_copy(s, d).wait_send()
        for turn in range(2):
            x_of = xx if turn % 2 == 0 else 1 - xx
            for a in range(per // 4):
                slot = 4 * a + 2 * x_of + core
                if turn == 0:
                    cross_copy(s, slot).wait_send()
                core_copy(s, slot).wait_send()

    def update_copy(i, j):
        return copy_to(
            update_out.at[j, i], update_in.at[blk, i], upd_send.at[j, i], upd_recv.at[blk, i], row, at_blk(j)
        )

    def update_wait(i, j):
        src = at_blk(j)
        return copy_to(
            update_out.at[j, i], update_in.at[src, i], upd_send.at[j, i], upd_recv.at[src, i], row, src
        )

    def pixel_part(i):
        return pl.ds(pl.multiple_of(i * cu, cu), cu)

    def update_out_stage(s, add):
        def body(i, carry):
            cols = pixel_part(i)
            term = dot_t(solved_full[...], panel[s, cols, :])
            if add:
                term = term + total[:, cols]
            total[:, cols] = term
            for j in range(1, n_blk):
                theirs = pl.ds(pl.multiple_of(at_blk(j) * dates, dates), dates)
                update_out[j, i] = total[theirs, cols].astype(BF16)
                update_copy(i, j).start()
            return carry
        lax.fori_loop(0, n_upd, body, 0)

    def reduced_part(i):
        cols = pixel_part(i)
        value = right_ref[:, cols] - total[my_dates, cols]
        for j in range(1, n_blk):
            update_wait(i, j).wait_recv()
            value = value - update_in[at_blk(j), i].astype(F32)
        reduced_ref[:, cols] = value
        return value

    @pl.when(row == 0)
    def _():
        lax.fori_loop(0, chunks, lambda i, c: (side_start(0, i), c)[1], 0)

    inverse_start(0)

    side_stage(0)
    solve_stage(0)

    @pl.when(row == 0)
    def _():
        load.wait()
        reduced_ref[...] = right_ref[...]

    @pl.when(row == 1)
    def _():
        update_out_stage(0, False)

        def body(i, carry):
            side[1, i] = reduced_part(i).astype(BF16)
            side_start(1, i)
            return carry
        lax.fori_loop(0, n_upd, body, 0)

    @pl.when(row > 1)
    def _():
        def body(i, carry):
            cols = pixel_part(i)
            total[:, cols] = dot_t(solved_full[...], panel[0, cols, :])
            return carry
        lax.fori_loop(0, n_upd, body, 0)

    side_stage(1)
    solve_stage(1)

    @pl.when(row > 1)
    def _():
        update_out_stage(1, True)

        def body(i, carry):
            reduced_part(i)
            return carry
        lax.fori_loop(0, n_upd, body, 0)

    for s in range(steps):
        inverse_finish(s)
        side_finish(s)
        solve_finish(s)

    @pl.when(row > 0)
    def _():
        def body(i, carry):
            for j in range(1, n_blk):
                update_copy(i, j).wait_send()
            return carry
        lax.fori_loop(0, n_upd, body, 0)


def solution(mesh):
    n_row, n_blk = mesh.shape["row"], mesh.shape["blk"]

    def local(factor_panel, right_side, block_inverse):
        pixels, steps, group = factor_panel.shape
        dates = right_side.shape[0]
        width = block_inverse.shape[1]
        order = group * n_blk
        cw = min(256, group)
        chunks = order // cw
        cu, cs = cw, 128
        n_upd = pixels // cu
        per, line = n_row // n_blk, n_row // 4
        dma = pltpu.SemaphoreType.DMA
        return pl.pallas_call(
            functools.partial(kernel, n_row, n_blk, cw, cu, cs),
            out_shape=(
                jax.ShapeDtypeStruct((steps, dates, width), F32),
                jax.ShapeDtypeStruct((dates, pixels), F32),
            ),
            in_specs=[
                pl.BlockSpec(memory_space=pl.ANY),
                pl.BlockSpec(memory_space=pltpu.VMEM),
                pl.BlockSpec(memory_space=pltpu.VMEM),
            ],
            out_specs=(
                pl.BlockSpec(memory_space=pltpu.VMEM),
                pl.BlockSpec(memory_space=pltpu.VMEM),
            ),
            scratch_shapes=[
                pltpu.VMEM((pixels, steps, group), BF16),
                pltpu.VMEM((steps, pixels, group), BF16),
                pltpu.VMEM((steps, width, group), BF16),
                pltpu.VMEM((steps, n_blk, width, group), BF16),
                pltpu.VMEM((steps, chunks, dates, cw), BF16),
                pltpu.VMEM((steps, dates, width), BF16),
                pltpu.VMEM((steps, per, n_blk * dates, width), BF16),
                pltpu.VMEM((n_blk * dates, group), BF16),
                pltpu.VMEM((n_blk * dates, pixels), F32),
                pltpu.VMEM((n_blk, n_upd, dates, cu), BF16),
                pltpu.VMEM((n_blk, n_upd, dates, cu), BF16),
                dma,
                dma((steps, n_blk)),
                dma((steps, n_blk)),
                dma((steps, chunks, 3)),
                dma((steps, chunks)),
                dma((steps,)),
                dma((steps, n_blk)),
                dma((steps, line)),
                dma((steps, per)),
                dma((steps, per)),
                dma((steps, per)),
                dma((n_blk, n_upd)),
                dma((n_blk, n_upd)),
            ],
            compiler_params=pltpu.CompilerParams(
                collective_id=0, has_side_effects=True, vmem_limit_bytes=48 << 20
            ),
        )(factor_panel, right_side, block_inverse)

    return jax.shard_map(
        local,
        mesh=mesh,
        in_specs=(P("row", None, "blk"), P("blk", "row"), P(None, "row", "blk")),
        out_specs=(P(None, "blk", "row"), P("blk", "row")),
        check_vma=False,
    )
```

```python
import functools

import jax
import jax.numpy as jnp
from jax import lax
from jax.experimental import pallas as pl
from jax.experimental.pallas import tpu as pltpu
from jax.sharding import PartitionSpec as P

MESH = pl.DeviceIdType.MESH
BF16 = jnp.bfloat16
F32 = jnp.float32


def dot_t(a, b):
    return lax.dot_general(a, b, (((1,), (1,)), ((), ())), preferred_element_type=F32)


def kernel(
    n_row, n_blk, cw, cu, cs,
    panel_hbm, right_ref, inverse_ref,
    solved_ref, reduced_ref,
    panel_raw, panel, own_inverse, inverse, side, own_solved, blocks, solved_full, total,
    update_out, update_in,
    panel_sem, inv_send, inv_recv, side_send, side_recv,
    hop_send, hop_recv, line_send, cross_send, core_send, block_recv, upd_send, upd_recv,
):
    row, blk = lax.axis_index("row"), lax.axis_index("blk")
    dates, pixels = right_ref.shape
    steps, width, group = inverse_ref.shape
    chunks = side.shape[1]
    per = n_row // n_blk
    line = n_row // 4
    zz, xx, core = row // 4, lax.rem(row // 2, 2), lax.rem(row, 2)
    chip = row // 2
    cross_row = row + 2 - 4 * xx
    core_row = row + 1 - 2 * core
    my_group = row // per
    my_slot = lax.rem(row, per)
    my_dates = pl.ds(pl.multiple_of(blk * dates, dates), dates)
    n_upd = pixels // cu

    def at_blk(j):
        return lax.rem(blk + j, n_blk)

    def copy_to(src, dst, send, recv, to_row, to_blk):
        return pltpu.make_async_remote_copy(
            src_ref=src, dst_ref=dst, send_sem=send, recv_sem=recv,
            device_id=(to_row, to_blk), device_id_type=MESH,
        )

    load = pltpu.make_async_copy(panel_hbm, panel_raw, panel_sem)
    load.start()

    barrier = pltpu.get_barrier_semaphore()

    def greet(to_row, to_blk):
        pl.semaphore_signal(barrier, inc=1, device_id=(to_row, to_blk), device_id_type=MESH)

    greet(core_row, blk)
    greet(cross_row, blk)
    for d in range(1, line):
        greet(lax.rem(row + 4 * d, n_row), blk)
    for j in range(1, n_blk):
        greet(row, at_blk(j))

    for s in range(steps):
        own_inverse[s] = inverse_ref[s].astype(BF16)

    @pl.when(row == 0)
    def _():
        for i in range(chunks):
            side[0, i] = right_ref[:, i * cw:(i + 1) * cw].astype(BF16)

    pl.semaphore_wait(barrier, 1 + 1 + (line - 1) + (n_blk - 1))

    def holds(j):
        return j * group < 2 * width * (chip + 1)

    def inverse_start(s):
        for j in range(1, n_blk):
            @pl.when(holds(blk))
            def _():
                inverse_copy(s, j).start()

    def inverse_finish(s):
        for j in range(1, n_blk):
            @pl.when(holds(blk))
            def _():
                inverse_copy(s, j).wait_send()

    def inverse_arrive(s):
        for j in range(1, n_blk):
            @pl.when(holds(at_blk(j)))
            def _():
                inverse_wait(s, j).wait_recv()

    def inverse_copy(s, j):
        return copy_to(
            own_inverse.at[s], inverse.at[s, blk], inv_send.at[s, j], inv_recv.at[s, blk], row, at_blk(j)
        )

    def inverse_wait(s, j):
        return copy_to(
            own_inverse.at[s], inverse.at[s, at_blk(j)], inv_send.at[s, j], inv_recv.at[s, at_blk(j)],
            row, at_blk(j),
        )

    def needs(chip_of, i):
        return i * cw < 2 * width * (chip_of + 1)

    def side_sends(s, i):
        half = lax.rem(i, 2)
        lane = core == s
        own = xx == half
        ref, recv = side.at[s, i], side_recv.at[s, i]
        down = copy_to(ref, ref, side_send.at[s, i, 0], recv, lax.rem(row + 4, n_row), blk)
        across = copy_to(ref, ref, side_send.at[s, i, 1], recv, cross_row, blk)
        over = copy_to(ref, ref, side_send.at[s, i, 2], recv, core_row, blk)
        there = own & (chip != 1) & needs(chip + 1 - 2 * xx, i)
        return (
            (lane & own & (zz < line - 1), down),
            (lane & (there | ((chip == 0) & jnp.logical_not(own))), across),
            (lane & needs(chip, i), over),
        )

    def side_start(s, i):
        for need, copy in side_sends(s, i):
            @pl.when(need)
            def _():
                copy.start()

    def side_finish(s):
        def body(i, carry):
            for need, copy in side_sends(s, i):
                @pl.when(need)
                def _():
                    copy.wait_send()
            return carry
        lax.fori_loop(0, chunks, body, 0)

    def side_wait(s, i):
        copy_to(side.at[s, i], side.at[s, i], side_send.at[s, i, 0], side_recv.at[s, i], core_row, blk).wait_recv()

    def split(s, i):
        rows = pl.ds(pl.multiple_of(i * cs, cs), cs)
        pair = panel_raw[rows].reshape(2 * cs, group)
        r = lax.broadcasted_iota(jnp.int32, (cs, 2 * cs), 0)
        c = lax.broadcasted_iota(jnp.int32, (cs, 2 * cs), 1)
        pick = jnp.where(c == 2 * r + s, 1.0, 0.0).astype(BF16)
        panel[s, rows, :] = jnp.dot(pick, pair, preferred_element_type=F32).astype(BF16)

    n_split = pixels // cs // chunks

    def side_stage(s):
        def turn(own):
            def body(m, carry):
                i = 2 * m + (xx if own else 1 - xx)
                lane = core == s
                due = needs(chip, i) | (lane if own else False)

                @pl.when((row != s) & due)
                def _():
                    side_wait(s, i)
                    side_start(s, i)

                @pl.when(row > s)
                def _():
                    if s == 0 and own:
                        @pl.when(m == 0)
                        def _():
                            load.wait()
                    base = (m if own else m + chunks // 2) * n_split
                    for k in range(n_split):
                        split(s, base + k)
                return carry
            lax.fori_loop(0, chunks // 2, body, 0)
        turn(True)
        turn(False)

    def hop(s):
        return copy_to(
            own_solved.at[s], blocks.at[s, my_slot, my_dates], hop_send.at[s], hop_recv.at[s, blk], row, my_group
        )

    def hop_in(s, j):
        src = at_blk(j)
        where = pl.ds(pl.multiple_of(src * dates, dates), dates)
        return copy_to(
            own_solved.at[s], blocks.at[s, my_slot, where], hop_send.at[s], hop_recv.at[s, src], row, src
        )

    def block_copy(s, slot, send, to_row):
        ref = blocks.at[s, slot]
        return copy_to(ref, ref, send, block_recv.at[s, slot], to_row, blk)

    def line_copies(s, slot):
        origin = (blk * per + slot) // 4
        return (
            ((zz >= origin) & (zz < line - 1),
             block_copy(s, slot, line_send.at[s, slot, 0], lax.rem(row + 4, n_row))),
            ((zz <= origin) & (zz > 0),
             block_copy(s, slot, line_send.at[s, slot, 1], lax.rem(row + n_row - 4, n_row))),
        )

    def line_start(s, slot):
        for need, copy in line_copies(s, slot):
            @pl.when(need)
            def _():
                copy.start()

    def cross_copy(s, slot):
        return block_copy(s, slot, cross_send.at[s, slot], cross_row)

    def core_copy(s, slot):
        return block_copy(s, slot, core_send.at[s, slot], core_row)

    def solve_stage(s):
        inverse_arrive(s)
        inverse[s, blk] = own_inverse[s]
        solved_ref[s] = jnp.zeros((dates, width), F32)
        for i in range(chunks):
            at, off = (i * cw) // group, (i * cw) % group

            @pl.when(needs(chip, i))
            def _():
                solved_ref[s] = solved_ref[s] + dot_t(side[s, i], inverse[s, at, :, off:off + cw])
        half = solved_ref[s].astype(BF16)

        @pl.when(blk != my_group)
        def _():
            own_solved[s] = half
            hop(s).start()

        @pl.when(blk == my_group)
        def _():
            blocks[s, my_slot, my_dates] = half

        if s + 1 < steps:
            inverse_start(s + 1)

        @pl.when(blk == my_group)
        def _():
            for j in range(1, n_blk):
                hop_in(s, j).wait_recv()
            line_start(s, my_slot)
            cross_copy(s, my_slot).start()
            core_copy(s, my_slot).start()

        for turn in range(4):
            x_of = xx if turn % 2 == 0 else 1 - xx
            c_of = core if turn < 2 else 1 - core
            for a in range(per // 4):
                near = jnp.where(zz > blk * (per // 4), per // 4 - 1 - a, a)
                slot = 4 * near + 2 * x_of + c_of
                mine = (blk == my_group) & (slot == my_slot)

                @pl.when(jnp.logical_not(mine))
                def _():
                    block_copy(s, slot, core_send.at[s, slot], core_row).wait_recv()
                    if turn == 0:
                        line_start(s, slot)
                        cross_copy(s, slot).start()
                    if turn < 2:
                        core_copy(s, slot).start()
        solved_full[...] = jnp.concatenate([blocks[s, t] for t in range(per)], axis=1)

    def solve_finish(s):
        @pl.when(blk != my_group)
        def _():
            hop(s).wait_send()

        for turn in range(2):
            x_of = xx if turn % 2 == 0 else 1 - xx
            for a in range(per // 4):
                slot = 4 * a + 2 * x_of + core
                if turn == 0:
                    for need, copy in line_copies(s, slot):
                        @pl.when(need)
                        def _():
                            copy.wait_send()
                    cross_copy(s, slot).wait_send()
                core_copy(s, slot).wait_send()

    def update_copy(i, j):
        return copy_to(
            update_out.at[j, i], update_in.at[blk, i], upd_send.at[j, i], upd_recv.at[blk, i], row, at_blk(j)
        )

    def update_wait(i, j):
        src = at_blk(j)
        return copy_to(
            update_out.at[j, i], update_in.at[src, i], upd_send.at[j, i], upd_recv.at[src, i], row, src
        )

    def pixel_part(i):
        return pl.ds(pl.multiple_of(i * cu, cu), cu)

    def update_out_stage(s, add):
        def body(i, carry):
            cols = pixel_part(i)
            term = dot_t(solved_full[...], panel[s, cols, :])
            if add:
                term = term + total[:, cols]
            total[:, cols] = term
            for j in range(1, n_blk):
                theirs = pl.ds(pl.multiple_of(at_blk(j) * dates, dates), dates)
                update_out[j, i] = total[theirs, cols].astype(BF16)
                update_copy(i, j).start()
            return carry
        lax.fori_loop(0, n_upd, body, 0)

    def reduced_part(i):
        cols = pixel_part(i)
        value = right_ref[:, cols] - total[my_dates, cols]
        for j in range(1, n_blk):
            update_wait(i, j).wait_recv()
            value = value - update_in[at_blk(j), i].astype(F32)
        reduced_ref[:, cols] = value
        return value

    @pl.when(row == 0)
    def _():
        lax.fori_loop(0, chunks, lambda i, c: (side_start(0, i), c)[1], 0)

    inverse_start(0)

    side_stage(0)
    solve_stage(0)

    @pl.when(row == 0)
    def _():
        load.wait()
        reduced_ref[...] = right_ref[...]

    @pl.when(row == 1)
    def _():
        update_out_stage(0, False)

        def body(i, carry):
            side[1, i] = reduced_part(i).astype(BF16)
            side_start(1, i)
            return carry
        lax.fori_loop(0, n_upd, body, 0)

    @pl.when(row > 1)
    def _():
        def body(i, carry):
            cols = pixel_part(i)
            total[:, cols] = dot_t(solved_full[...], panel[0, cols, :])
            return carry
        lax.fori_loop(0, n_upd, body, 0)

    side_stage(1)
    solve_stage(1)

    @pl.when(row > 1)
    def _():
        update_out_stage(1, True)

        def body(i, carry):
            reduced_part(i)
            return carry
        lax.fori_loop(0, n_upd, body, 0)

    for s in range(steps):
        inverse_finish(s)
        side_finish(s)
        solve_finish(s)

    @pl.when(row > 0)
    def _():
        def body(i, carry):
            for j in range(1, n_blk):
                update_copy(i, j).wait_send()
            return carry
        lax.fori_loop(0, n_upd, body, 0)


def solution(mesh):
    n_row, n_blk = mesh.shape["row"], mesh.shape["blk"]

    def local(factor_panel, right_side, block_inverse):
        pixels, steps, group = factor_panel.shape
        dates = right_side.shape[0]
        width = block_inverse.shape[1]
        order = group * n_blk
        cw = min(256, group)
        chunks = order // cw
        cu, cs = cw, 128
        n_upd = pixels // cu
        per, line = n_row // n_blk, n_row // 4
        dma = pltpu.SemaphoreType.DMA
        return pl.pallas_call(
            functools.partial(kernel, n_row, n_blk, cw, cu, cs),
            out_shape=(
                jax.ShapeDtypeStruct((steps, dates, width), F32),
                jax.ShapeDtypeStruct((dates, pixels), F32),
            ),
            in_specs=[
                pl.BlockSpec(memory_space=pl.ANY),
                pl.BlockSpec(memory_space=pltpu.VMEM),
                pl.BlockSpec(memory_space=pltpu.VMEM),
            ],
            out_specs=(
                pl.BlockSpec(memory_space=pltpu.VMEM),
                pl.BlockSpec(memory_space=pltpu.VMEM),
            ),
            scratch_shapes=[
                pltpu.VMEM((pixels, steps, group), BF16),
                pltpu.VMEM((steps, pixels, group), BF16),
                pltpu.VMEM((steps, width, group), BF16),
                pltpu.VMEM((steps, n_blk, width, group), BF16),
                pltpu.VMEM((steps, chunks, dates, cw), BF16),
                pltpu.VMEM((steps, dates, width), BF16),
                pltpu.VMEM((steps, per, n_blk * dates, width), BF16),
                pltpu.VMEM((n_blk * dates, group), BF16),
                pltpu.VMEM((n_blk * dates, pixels), F32),
                pltpu.VMEM((n_blk, n_upd, dates, cu), BF16),
                pltpu.VMEM((n_blk, n_upd, dates, cu), BF16),
                dma,
                dma((steps, n_blk)),
                dma((steps, n_blk)),
                dma((steps, chunks, 3)),
                dma((steps, chunks)),
                dma((steps,)),
                dma((steps, n_blk)),
                dma((steps, per, 2)),
                dma((steps, per)),
                dma((steps, per)),
                dma((steps, per)),
                dma((n_blk, n_upd)),
                dma((n_blk, n_upd)),
            ],
            compiler_params=pltpu.CompilerParams(
                collective_id=0, has_side_effects=True, vmem_limit_bytes=48 << 20
            ),
        )(factor_panel, right_side, block_inverse)

    return jax.shard_map(
        local,
        mesh=mesh,
        in_specs=(P("row", None, "blk"), P("blk", "row"), P(None, "row", "blk")),
        out_specs=(P(None, "blk", "row"), P("blk", "row")),
        check_vma=False,
    )
```
